32 devices in a mesh: pole: 2 (over x), row: 16 (over z, y, core).
Axes of the slice: x: 2, y: 2, z: 4, core: 2. Of those that a mesh axis runs over, the one named last changes fastest.
Arguments:
- inverse_root: bfloat16 [8192, 4096], P(('pole', 'row')), parts along dimension 0
- lower_panel: bfloat16 [8192, 512], P(('pole', 'row')), parts along dimension 0, may hold values from -0.3984375 to 0.3984375
- coupling: int32 [16], replicated, may hold values from 0 to 2
- child_inverse: float32 [1024, 256], P(('pole', 'row')), parts along dimension 0, may hold values from -3 to 3
Outputs:
- offdiag: float32 [8192, 512], P(('pole', 'row')), parts along dimension 0
- child_diag: float32 [1024, 256], P(('pole', 'row')), parts along dimension 0
The draws below stay inside these ranges and needn't reach their ends.
There are 2 independent parts, one for each index of `pole`. The reference program is written for one: setup_inputs(seed, part) draws one part's arguments, and reference() takes and returns one part's arrays. A program takes and returns all parts, laid end to end along the dimension named above; an argument that names none is the same for every part. Nothing has to cross between parts.
Inputs may be any that keep to these rules, and one draw needn't show every extreme that they name: `coupling`: entry t names the child supernode coupled to tile row t of the separator; the value 2 means that the tile row couples to no child.
All inputs are finite; a program needn't handle non-finite values.
Results may differ from the reference program's by a relative error of at most 0.0003.
Values may be sent and summed in bfloat16 or wider, within the bound.
No kernel may reach another device: no remote copies, remote signals or barrier semaphores. Data moves between devices by JAX's collectives and lax.ppermute only.
A program may use at most 64 MiB of HBM per device.

```python
import jax
import jax.numpy as jnp
from jax import lax

B = 256
NCH = 2
NR = 4096
CW = 256
NC = 512


def draw_inverse_root(key, part):
    key = jax.random.fold_in(key, 11)
    first, second = jax.random.split(key)
    spread = jax.random.normal(first, (NR, NR), jnp.float32)
    pivots = jax.random.uniform(second, (NR,), jnp.float32, 1.0, 2.0)
    ident = jnp.arange(NR)[:, None] == jnp.arange(NR)[None, :]
    whole = 0.5 / NR ** 0.5 * spread + jnp.where(ident, pivots[:, None], jnp.float32(0.0))
    return whole.astype(jnp.bfloat16)


def set_ends(result, key, low, top_value):
    extent = result.shape
    place = [jax.random.randint(jax.random.fold_in(key, axis), (), 0, extent[axis]) for axis in range(len(extent))]
    result = result.at[tuple(place)].set(low)
    longest = extent.index(max(extent))
    place[longest] = (place[longest] + 1) % extent[longest]
    return result.at[tuple(place)].set(top_value)


def level_of(key, dims, pieces, least, top_value):
    def one(axis_at, shards_of):
        heights = jax.random.uniform(jax.random.fold_in(jax.random.fold_in(key, 6), axis_at), (shards_of,), jnp.float32, least / len(pieces), top_value / len(pieces))
        return jnp.repeat(jnp.exp(heights), dims[axis_at] // shards_of).reshape((-1,) + (1,) * (len(dims) - axis_at - 1))

    factor_of = one(*pieces[0])
    for cut in pieces[1:]:
        factor_of = factor_of * one(*cut)
    return factor_of


def gaussian(key, dims, scale, bound, cuts=(), kind=jnp.bfloat16):
    entries = jax.random.normal(key, dims, jnp.float32) * scale
    if len(cuts) > 0:
        entries = level_of(key, dims, cuts, -0.22, 0.18) * entries
    return jnp.clip(entries, min=-bound, max=bound).astype(kind)


def setup_inputs(seed: int = 0, part: int = 0) -> dict:
    keys = jax.random.split(jax.random.key(seed), 5)
    part_splits = jax.random.split(jax.random.fold_in(keys[4], part), 5)
    return {
        "inverse_root": draw_inverse_root(jax.random.fold_in(jax.random.fold_in(keys[4], part), 71), part),
        "lower_panel": gaussian(part_splits[1], (NR, NC), 0.05, 0.3984375, ((0, 16),)),
        "coupling": set_ends(jax.random.randint(keys[2], (NR // B,), 0, NCH + 1), jax.random.fold_in(keys[2], 1), 0, NCH).astype(jnp.int32),
        "child_inverse": gaussian(part_splits[3], (NC, CW), 0.5, 3.0, ((0, 16),), jnp.float32),
    }


def reference(inverse_root, lower_panel, coupling, child_inverse):
    rows_all = inverse_root.shape[0]
    width = lower_panel.shape[1]
    col_child = (jnp.arange(width) // CW).astype(jnp.int32)
    row_child = jnp.repeat(coupling, B)
    pattern = row_child[:, None] == col_child[None, :]
    panel = jnp.where(pattern, lower_panel, jnp.zeros_like(lower_panel))
    product = jnp.dot(inverse_root, panel, preferred_element_type=jnp.float32)
    offdiag = jnp.where(pattern, -product, jnp.float32(0.0))
    blocks = []
    for child in range(NCH):
        left = panel[:, child * CW:(child + 1) * CW].astype(jnp.float32)
        right = offdiag[:, child * CW:(child + 1) * CW]
        blocks.append(jnp.dot(left.T, right, precision=lax.Precision.HIGHEST, preferred_element_type=jnp.float32))
    child_diag = child_inverse - jnp.concatenate(blocks, axis=0)
    return offdiag, child_diag
```

```python
import functools

import jax
import jax.numpy as jnp
from jax import lax
from jax.experimental import pallas as pl
from jax.experimental.pallas import tpu as pltpu
from jax.sharding import PartitionSpec as P

NCH = 2
CW = 256


def exchange(block, n, mask):
    return lax.ppermute(block, "row", [(i, i ^ mask) for i in range(n)])


def compact_kernel(coupling_ref, panel_ref, block_ref):
    child = coupling_ref[lax.axis_index("row")]
    start = pl.multiple_of(jnp.minimum(child, NCH - 1) * CW, CW)
    block_ref[...] = panel_ref[:, pl.ds(start, CW)]


def product_kernel(n, coupling_ref, inverse_ref, *refs):
    block_refs = refs[:n]
    offdiag_ref, send_ref, keep_ref, total = refs[n:]
    rows = inverse_ref.shape[0]
    me = lax.axis_index("row")
    child = coupling_ref[me]
    total[...] = jnp.zeros_like(total)
    for offset in range(n):
        tile = me ^ offset

        @pl.when((coupling_ref[tile] == child) & (child < NCH))
        def _():
            start = pl.multiple_of(tile * rows, rows)
            total[...] += jnp.dot(
                inverse_ref[:, pl.ds(start, rows)],
                block_refs[offset][...],
                preferred_element_type=jnp.float32,
            )

    product = total[...]
    zero = jnp.zeros_like(product)
    for k in range(NCH):
        offdiag_ref[:, k * CW:(k + 1) * CW] = jnp.where(child == k, -product, zero)
    left = block_refs[0][...]
    term = zero
    rest = product
    for _ in range(3):
        part = rest.astype(jnp.bfloat16)
        rest = rest - part.astype(jnp.float32)
        term += lax.dot_general(
            left, part, (((0,), (0,)), ((), ())), preferred_element_type=jnp.float32
        )
    piece = NCH * CW // n
    core = lax.rem(me, 2)
    for q in range(CW // piece // 2):
        low = term[2 * q * piece:(2 * q + 1) * piece]
        high = term[(2 * q + 1) * piece:(2 * q + 2) * piece]
        keep_ref[q * piece:(q + 1) * piece] = jnp.where(core == 0, low, high)
        send_ref[q * piece:(q + 1) * piece] = jnp.where(core == 0, high, low)


def pieces_kernel(n, coupling_ref, keep_ref, got_ref, *out_refs):
    piece = NCH * CW // n
    per_child = n // NCH // 2
    me = lax.axis_index("row")
    mine = coupling_ref[me]
    other = coupling_ref[me ^ 1]
    for offset in range(n // 2):
        place = lax.div(me ^ (2 * offset), 2)
        child = lax.div(place, per_child)
        start = pl.multiple_of(lax.rem(place, per_child) * piece, piece)
        kept = keep_ref[pl.ds(start, piece)]
        got = got_ref[pl.ds(start, piece)]
        zero = jnp.zeros_like(kept)
        out_refs[offset][...] = jnp.where(mine == child, kept, zero) + jnp.where(
            other == child, got, zero
        )


def per_device(n, inverse_root, lower_panel, coupling, child_inverse):
    rows = inverse_root.shape[0]
    smem = pl.BlockSpec(memory_space=pltpu.SMEM)
    vmem = pl.BlockSpec(memory_space=pltpu.VMEM)
    block = pl.pallas_call(
        compact_kernel,
        out_shape=jax.ShapeDtypeStruct((rows, CW), lower_panel.dtype),
        in_specs=[smem, vmem],
        out_specs=vmem,
        name="compact",
    )(coupling, lower_panel)
    held = {0: block}
    for offset in sorted(range(1, n), key=lambda o: (o.bit_count(), -o)):
        mask = offset & -offset
        held[offset] = exchange(held[offset ^ mask], n, mask)
    offdiag, send, keep = pl.pallas_call(
        functools.partial(product_kernel, n),
        out_shape=[
            jax.ShapeDtypeStruct((rows, NCH * CW), jnp.float32),
            jax.ShapeDtypeStruct((CW // 2, CW), jnp.float32),
            jax.ShapeDtypeStruct((CW // 2, CW), jnp.float32),
        ],
        in_specs=[smem] + [vmem] * (n + 1),
        out_specs=[vmem] * 3,
        scratch_shapes=[pltpu.VMEM((rows, CW), jnp.float32)],
        compiler_params=pltpu.CompilerParams(vmem_limit_bytes=48 * 2**20),
        name="product",
    )(coupling, inverse_root, *[held[offset] for offset in range(n)])
    got = exchange(send, n, 1)
    piece = NCH * CW // n
    parts = pl.pallas_call(
        functools.partial(pieces_kernel, n),
        out_shape=[jax.ShapeDtypeStruct((piece, CW), jnp.float32)] * (n // 2),
        in_specs=[smem, vmem, vmem],
        out_specs=[vmem] * (n // 2),
        name="pieces",
    )(coupling, keep, got)
    child_diag = child_inverse + parts[0]
    for offset in range(1, n // 2):
        child_diag = child_diag + exchange(parts[offset], n, 2 * offset)
    return offdiag, child_diag


def solution(mesh):
    split = P(("pole", "row"), None)
    return jax.shard_map(
        functools.partial(per_device, mesh.shape["row"]),
        mesh=mesh,
        in_specs=(split, split, P(), split),
        out_specs=(split, split),
        check_vma=False,
    )
```

```python
import functools

import jax
import jax.numpy as jnp
from jax import lax
from jax.experimental import pallas as pl
from jax.experimental.pallas import tpu as pltpu
from jax.sharding import PartitionSpec as P

NCH = 2
CW = 256
MIB = 2**20
QUAD = ((0, 0), (1, 2), (2, 1), (3, 3))
SMEM = pl.BlockSpec(memory_space=pltpu.SMEM)
VMEM = pl.BlockSpec(memory_space=pltpu.VMEM)
ANY = pl.BlockSpec(memory_space=pl.ANY)


def params(mib):
    return pltpu.CompilerParams(vmem_limit_bytes=mib * MIB)


def exchange(block, n, masks):
    return lax.ppermute(block, "row", [(i, i ^ masks[i % 2]) for i in range(n)])


def compact_kernel(coupling_ref, panel_ref, block_ref):
    child = coupling_ref[lax.axis_index("row")]
    start = pl.multiple_of(jnp.minimum(child, NCH - 1) * CW, CW)
    block_ref[...] = panel_ref[:, pl.ds(start, CW)]


def load_kernel(inverse_hbm, after_ref, inverse_ref, sem):
    copy = pltpu.make_async_copy(inverse_hbm, inverse_ref, sem)
    copy.start()
    copy.wait()


def after_kernel(block_ref, after_ref, out_ref):
    out_ref[...] = block_ref[...]


def join_kernel(low_ref, high_ref, after_ref, out_ref):
    rows = low_ref.shape[0]
    out_ref[:rows] = low_ref[...]
    out_ref[rows:] = high_ref[...]


def late_kernel(n, places, coupling_ref, inverse_ref, *refs):
    rows = inverse_ref.shape[0]
    block_refs = refs[:-4]
    product_ref, send_ref, keep_ref, flag_ref = refs[-4:]
    me = lax.axis_index("row")
    core = lax.rem(me, 2)
    child = coupling_ref[me]
    other = coupling_ref[me ^ 1]
    product_ref[...] = jnp.zeros_like(product_ref)
    for held, block_ref in zip(places, block_refs):
        for number, (even, odd) in enumerate(held):
            tile = me ^ jnp.where(core == 0, even, odd)

            @pl.when((coupling_ref[tile] == child) & (child < NCH))
            def _():
                start = pl.multiple_of(tile * rows, rows)
                product_ref[...] += jnp.dot(
                    inverse_ref[:, pl.ds(start, rows)],
                    block_ref[number * rows:(number + 1) * rows],
                    preferred_element_type=jnp.float32,
                )

    left = block_refs[0][...]
    rest = product_ref[...]
    term = jnp.zeros_like(rest)
    for _ in range(3):
        part = rest.astype(jnp.bfloat16)
        rest = rest - part.astype(jnp.float32)
        term += lax.dot_general(
            left, part, (((0,), (0,)), ((), ())), preferred_element_type=jnp.float32
        )
    piece = NCH * CW // n
    for q in range(CW // piece // 2):
        low = term[2 * q * piece:(2 * q + 1) * piece]
        high = term[(2 * q + 1) * piece:(2 * q + 2) * piece]
        keep_ref[q * piece:(q + 1) * piece] = jnp.where(core == 0, low, high)
        send_ref[q * piece:(q + 1) * piece] = jnp.where(core == 0, high, low)
    for k in range(NCH):
        flag_ref[2 * k:2 * k + 1] = jnp.full((1, CW), jnp.where(child == k, 1.0, 0.0))
        flag_ref[2 * k + 1:2 * k + 2] = jnp.full(
            (1, CW), jnp.where(other == k, 1.0, 0.0)
        )


def offdiag_kernel(coupling_ref, product_ref, offdiag_ref):
    child = coupling_ref[lax.axis_index("row")]
    product = product_ref[...]
    for k in range(NCH):
        offdiag_ref[:, k * CW:(k + 1) * CW] = jnp.where(
            child == k, -product, jnp.zeros_like(product)
        )


def quad_kernel(piece, kept_ref, got_ref, flag_ref, *out_refs):
    me = lax.axis_index("row")
    core = lax.rem(me, 2)
    low = lax.rem(lax.div(me, 2), 4)
    groups = kept_ref.shape[0] // piece // 4
    for (even, odd), out_ref in zip(QUAD, out_refs):
        want = low ^ jnp.where(core == 0, even, odd)
        for child in range(NCH):
            for group in range(groups):
                start = pl.multiple_of((group * 4 + want) * piece, piece)
                kept = kept_ref[pl.ds(start, piece)]
                got = got_ref[pl.ds(start, piece)]
                zero = jnp.zeros_like(kept)
                at = (child * groups + group) * piece
                out_ref[at:at + piece] = jnp.where(
                    flag_ref[2 * child:2 * child + 1] > 0.5, kept, zero
                ) + jnp.where(flag_ref[2 * child + 1:2 * child + 2] > 0.5, got, zero)


def halve_kernel(piece, bit, *refs):
    part_refs, send_ref, keep_ref = refs[:-2], refs[-2], refs[-1]
    mine = lax.rem(lax.div(lax.axis_index("row"), 2 << bit), 2)
    for out_ref, side in ((keep_ref, mine), (send_ref, 1 - mine)):
        for index in range(out_ref.shape[0] // piece):
            rows = pl.ds(pl.multiple_of((2 * index + side) * piece, piece), piece)
            total = part_refs[0][rows]
            for part_ref in part_refs[1:]:
                total = total + part_ref[rows]
            out_ref[index * piece:(index + 1) * piece] = total


def last_kernel(inverse_ref, kept_ref, got_ref, diag_ref):
    diag_ref[...] = inverse_ref[...] + (kept_ref[...] + got_ref[...])


def gather(block, inverse_root, n):
    held = {"own": block}
    places = {"own": [(0, 0)]}

    def fetch(name, source, masks, block=None):
        held[name] = exchange(held[source] if block is None else block, n, masks)
        places[name] = [
            tuple(masks[c] ^ pair[c ^ (masks[0] & 1)] for c in range(2))
            for pair in places[source]
        ]

    def after(name, block):
        return pl.pallas_call(
            after_kernel,
            out_shape=pltpu.VMEM(block.shape, block.dtype),
            in_specs=[VMEM, ANY],
            out_specs=VMEM,
            compiler_params=params(2),
            name="after",
        )(block, held[name])

    fetch("d", "own", (8, 8))
    fetch("own1", "own", (1, 1))
    fetch("a", "own", (2, 4))
    inverse = pl.pallas_call(
        load_kernel,
        out_shape=pltpu.VMEM(inverse_root.shape, inverse_root.dtype),
        in_specs=[ANY, ANY],
        out_specs=VMEM,
        scratch_shapes=[pltpu.SemaphoreType.DMA],
        compiler_params=params(62 - inverse_root.size * 2 // MIB),
        name="load",
    )(inverse_root, held["own1"])
    pair = pl.pallas_call(
        join_kernel,
        out_shape=pltpu.VMEM((2 * block.shape[0], CW), block.dtype),
        in_specs=[VMEM, VMEM, ANY],
        out_specs=VMEM,
        compiler_params=params(2),
        name="join",
    )(block, held["a"], inverse)
    places["pair"] = places["own"] + places["a"]
    fetch("bc", "pair", (4, 2), pair)
    del places["pair"]
    fetch("a1", "a", (1, 1))
    fetch("d1", "d", (1, 1))
    fetch("f", "d", (2, 4))
    fetch("e", "d", (4, 2))
    fetch("g", "d", (6, 6), after("d1", held["d"]))
    for name in ("bc", "f", "e", "g"):
        fetch(name + "1", name, (1, 1))
    for bit in range(4, n.bit_length() - 1):
        for name in list(held):
            fetch(f"{name}_{bit}", name, (1 << bit, 1 << bit))
    held["inverse"] = inverse
    return held, places


def per_device(n, inverse_root, lower_panel, coupling, child_inverse):
    rows = inverse_root.shape[0]
    block = pl.pallas_call(
        compact_kernel,
        out_shape=pltpu.VMEM((rows, CW), lower_panel.dtype),
        in_specs=[SMEM, VMEM],
        out_specs=VMEM,
        compiler_params=params(60),
        name="compact",
    )(coupling, lower_panel)
    held, places = gather(block, inverse_root, n)
    inverse = held.pop("inverse")
    product, send, keep, flags = pl.pallas_call(
        functools.partial(late_kernel, n, list(places.values())),
        out_shape=[
            jax.ShapeDtypeStruct((rows, CW), jnp.float32),
            jax.ShapeDtypeStruct((CW // 2, CW), jnp.float32),
            jax.ShapeDtypeStruct((CW // 2, CW), jnp.float32),
            jax.ShapeDtypeStruct((8, CW), jnp.float32),
        ],
        in_specs=[SMEM] + [VMEM] * (len(held) + 1),
        out_specs=[VMEM] * 4,
        compiler_params=params(24 if n > 16 else 8),
        name="late",
    )(coupling, inverse, *held.values())
    got = exchange(send, n, (1, 1))
    offdiag = pl.pallas_call(
        offdiag_kernel,
        out_shape=jax.ShapeDtypeStruct((rows, NCH * CW), jnp.float32),
        in_specs=[SMEM, VMEM],
        out_specs=VMEM,
        compiler_params=params(2),
        name="offdiag",
    )(coupling, product)
    piece = NCH * CW // n
    width = NCH * CW // 2 // len(QUAD)
    parts = list(pl.pallas_call(
        functools.partial(quad_kernel, piece),
        out_shape=[jax.ShapeDtypeStruct((width, CW), jnp.float32)] * len(QUAD),
        in_specs=[VMEM] * 3,
        out_specs=[VMEM] * len(QUAD),
        compiler_params=params(2),
        name="quad",
    )(keep, got, flags))
    for number in range(1, len(QUAD)):
        parts[number] = exchange(parts[number], n, tuple(2 * m for m in QUAD[number]))
    for bit in range(2, (n // 2).bit_length() - 1):
        width //= 2
        send, keep = pl.pallas_call(
            functools.partial(halve_kernel, piece, bit),
            out_shape=[jax.ShapeDtypeStruct((width, CW), jnp.float32)] * 2,
            in_specs=[VMEM] * len(parts),
            out_specs=[VMEM] * 2,
            compiler_params=params(2),
            name=f"halve{bit}",
        )(*parts)
        got = exchange(send, n, (2 << bit, 2 << bit))
        parts = [keep, got]
    child_diag = pl.pallas_call(
        last_kernel,
        out_shape=jax.ShapeDtypeStruct((piece, CW), jnp.float32),
        in_specs=[VMEM] * 3,
        out_specs=VMEM,
        compiler_params=params(2),
        name="last",
    )(child_inverse, keep, got)
    return offdiag, child_diag


def solution(mesh):
    split = P(("pole", "row"), None)
    return jax.shard_map(
        functools.partial(per_device, mesh.shape["row"]),
        mesh=mesh,
        in_specs=(split, split, P(), split),
        out_specs=(split, split),
        check_vma=False,
    )
```

```python
import functools

import jax
import jax.numpy as jnp
from jax import lax
from jax.experimental import pallas as pl
from jax.experimental.pallas import tpu as pltpu
from jax.sharding import PartitionSpec as P

NCH = 2
CW = 256
MIB = 2**20
QUAD = ((0, 0), (1, 2), (2, 1), (3, 3))
SMEM = pl.BlockSpec(memory_space=pltpu.SMEM)
VMEM = pl.BlockSpec(memory_space=pltpu.VMEM)
ANY = pl.BlockSpec(memory_space=pl.ANY)
TOKEN = pltpu.VMEM((8, 128), jnp.float32)


def params(mib):
    return pltpu.CompilerParams(vmem_limit_bytes=mib * MIB)


def exchange(block, n, masks):
    return lax.ppermute(block, "row", [(i, i ^ masks[i % 2]) for i in range(n)])


def compact_kernel(coupling_ref, panel_ref, block_ref):
    child = coupling_ref[lax.axis_index("row")]
    start = pl.multiple_of(jnp.minimum(child, NCH - 1) * CW, CW)
    block_ref[...] = panel_ref[:, pl.ds(start, CW)]


def load_kernel(mine_hbm, other_hbm, mine_ref, other_ref, sems):
    rows = mine_hbm.shape[0]
    core = lax.rem(lax.axis_index("row"), 2)
    copies = []
    for pair in range(mine_ref.shape[1] // rows):
        here = pl.ds(pl.multiple_of((2 * pair + core) * rows, rows), rows)
        there = pl.ds(pair * rows, rows)
        for number, (source, ref) in enumerate(
            ((mine_hbm, mine_ref), (other_hbm, other_ref))
        ):
            copies.append(
                pltpu.make_async_copy(
                    source.at[:, here], ref.at[:, there], sems.at[pair, number]
                )
            )
    for copy in copies:
        copy.start()
    for copy in copies:
        copy.wait()


def after_kernel(block_ref, after_ref, out_ref):
    out_ref[...] = block_ref[...]


def join_kernel(low_ref, high_ref, after_ref, out_ref):
    rows = low_ref.shape[0]
    out_ref[:rows] = low_ref[...]
    out_ref[rows:] = high_ref[...]


def product_kernel(n, places, coupling_ref, mine_z, other_z, other_own, *refs):
    block_refs = refs[:-4]
    mine_ref, other_ref, send_ref, keep_ref = refs[-4:]
    rows = mine_z.shape[0]
    me = lax.axis_index("row")
    core = lax.rem(me, 2)
    children = (coupling_ref[me], coupling_ref[me ^ 1])
    for total_ref in (mine_ref, other_ref):
        total_ref[...] = jnp.zeros_like(total_ref)
    for held, block_ref in zip(places, block_refs):
        for number, (even, odd) in enumerate(held):
            tile = me ^ jnp.where(core == 0, even, odd)
            tile_child = coupling_ref[tile]
            columns = pl.ds(pl.multiple_of(lax.div(tile, 2) * rows, rows), rows)
            for child, z_ref, total_ref in zip(
                children, (mine_z, other_z), (mine_ref, other_ref)
            ):

                @pl.when((tile_child == child) & (child < NCH))
                def _():
                    total_ref[...] += jnp.dot(
                        z_ref[:, columns],
                        block_ref[number * rows:(number + 1) * rows],
                        preferred_element_type=jnp.float32,
                    )

    terms = []
    for left_ref, total_ref in ((block_refs[0], mine_ref), (other_own, other_ref)):
        total = total_ref[...]
        high = total.astype(jnp.bfloat16)
        low = (total - high.astype(jnp.float32)).astype(jnp.bfloat16)
        left = left_ref[...]
        terms.append(
            sum(
                lax.dot_general(
                    left, part, (((0,), (0,)), ((), ())), preferred_element_type=jnp.float32
                )
                for part in (high, low)
            )
        )
    piece = NCH * CW // n
    zero = jnp.zeros((piece, CW), jnp.float32)
    for child in range(NCH):
        for q in range(CW // piece // 2):
            low, high = [
                sum(
                    jnp.where(mine == child, term[at:at + piece], zero)
                    for mine, term in zip(children, terms)
                )
                for at in (2 * q * piece, (2 * q + 1) * piece)
            ]
            at = child * (CW // 2) + q * piece
            keep_ref[at:at + piece] = jnp.where(core == 0, low, high)
            send_ref[at:at + piece] = jnp.where(core == 0, high, low)


def offdiag_kernel(coupling_ref, mine_ref, other_ref, offdiag_ref, token_ref):
    token_ref[...] = jnp.zeros_like(token_ref)
    child = coupling_ref[lax.axis_index("row")]
    product = mine_ref[...] + other_ref[...]
    for k in range(NCH):
        offdiag_ref[:, k * CW:(k + 1) * CW] = jnp.where(
            child == k, -product, jnp.zeros_like(product)
        )


def quad_kernel(piece, kept_ref, got_ref, *out_refs):
    me = lax.axis_index("row")
    core = lax.rem(me, 2)
    low = lax.rem(lax.div(me, 2), 4)
    for (even, odd), out_ref in zip(QUAD, out_refs):
        want = low ^ jnp.where(core == 0, even, odd)
        for group in range(out_ref.shape[0] // piece):
            rows = pl.ds(pl.multiple_of((group * 4 + want) * piece, piece), piece)
            out_ref[group * piece:(group + 1) * piece] = kept_ref[rows] + got_ref[rows]


def halve_kernel(piece, bit, *refs):
    part_refs, send_ref, keep_ref = refs[:-2], refs[-2], refs[-1]
    mine = lax.rem(lax.div(lax.axis_index("row"), 2 << bit), 2)
    for out_ref, side in ((keep_ref, mine), (send_ref, 1 - mine)):
        for index in range(out_ref.shape[0] // piece):
            rows = pl.ds(pl.multiple_of((2 * index + side) * piece, piece), piece)
            total = part_refs[0][rows]
            for part_ref in part_refs[1:]:
                total = total + part_ref[rows]
            out_ref[index * piece:(index + 1) * piece] = total


def last_kernel(inverse_ref, kept_ref, got_ref, after_ref, diag_ref):
    diag_ref[...] = inverse_ref[...] + (kept_ref[...] + got_ref[...])


def after(block, other):
    return pl.pallas_call(
        after_kernel,
        out_shape=pltpu.VMEM(block.shape, block.dtype),
        in_specs=[VMEM, ANY],
        out_specs=VMEM,
        compiler_params=params(2),
        name="after",
    )(block, other)


def gather(block, inverse_root, n):
    rows = block.shape[0]
    held = {"own": ([(0, 0)], block)}

    def fetch(name, source, masks):
        tiles, held_block = held[source]
        held[name] = (
            [tuple(masks[c] ^ pair[c] for c in range(2)) for pair in tiles],
            exchange(held_block, n, masks),
        )

    fetch("d", "own", (8, 8))
    other_own = exchange(block, n, (1, 1))
    fetch("a", "own", (2, 4))
    other_z = exchange(lax.optimization_barrier((inverse_root, block))[0], n, (1, 1))
    half = pltpu.VMEM((rows, inverse_root.shape[1] // 2), inverse_root.dtype)
    mine_z, other_z = pl.pallas_call(
        load_kernel,
        out_shape=[half, half],
        in_specs=[ANY, ANY],
        out_specs=[VMEM] * 2,
        scratch_shapes=[pltpu.SemaphoreType.DMA((n // 2, 2))],
        compiler_params=params(62 - inverse_root.size * 2 // MIB),
        name="load",
    )(inverse_root, other_z)
    pair = pl.pallas_call(
        join_kernel,
        out_shape=pltpu.VMEM((2 * rows, CW), block.dtype),
        in_specs=[VMEM, VMEM, ANY],
        out_specs=VMEM,
        compiler_params=params(2),
        name="join",
    )(block, held["a"][1], mine_z)
    held["pair"] = (held["own"][0] + held["a"][0], pair)
    fetch("bc", "pair", (4, 2))
    del held["pair"]
    fetch("g", "d", (6, 6))
    fetch("f", "d", (2, 4))
    fetch("e", "d", (4, 2))
    for bit in range(4, n.bit_length() - 1):
        for name in list(held):
            fetch(f"{name}_{bit}", name, (1 << bit, 1 << bit))
    return mine_z, other_z, other_own, list(held.values())


def per_device(n, inverse_root, lower_panel, coupling, child_inverse):
    rows = inverse_root.shape[0]
    block = pl.pallas_call(
        compact_kernel,
        out_shape=pltpu.VMEM((rows, CW), lower_panel.dtype),
        in_specs=[SMEM, VMEM],
        out_specs=VMEM,
        compiler_params=params(60),
        name="compact",
    )(coupling, lower_panel)
    mine_z, other_z, other_own, held = gather(block, inverse_root, n)
    mine, other, send, keep = pl.pallas_call(
        functools.partial(product_kernel, n, [places for places, _ in held]),
        out_shape=[
            jax.ShapeDtypeStruct((rows, CW), jnp.float32),
            jax.ShapeDtypeStruct((rows, CW), jnp.float32),
            jax.ShapeDtypeStruct((NCH * CW // 2, CW), jnp.float32),
            jax.ShapeDtypeStruct((NCH * CW // 2, CW), jnp.float32),
        ],
        in_specs=[SMEM] + [VMEM] * (len(held) + 3),
        out_specs=[VMEM] * 4,
        compiler_params=params(24 if n > 16 else 8),
        name="product",
    )(coupling, mine_z, other_z, other_own, *[block for _, block in held])
    got = exchange(send, n, (1, 1))
    piece = NCH * CW // n
    width = NCH * CW // 2 // len(QUAD)
    parts = list(pl.pallas_call(
        functools.partial(quad_kernel, piece),
        out_shape=[jax.ShapeDtypeStruct((width, CW), jnp.float32)] * len(QUAD),
        in_specs=[VMEM] * 2,
        out_specs=[VMEM] * len(QUAD),
        compiler_params=params(2),
        name="quad",
    )(keep, got))
    offdiag, token = pl.pallas_call(
        offdiag_kernel,
        out_shape=[jax.ShapeDtypeStruct((rows, NCH * CW), jnp.float32), TOKEN],
        in_specs=[SMEM, VMEM, VMEM],
        out_specs=[VMEM] * 2,
        compiler_params=params(4),
        name="offdiag",
    )(coupling, mine, exchange(after(other, parts[0]), n, (1, 1)))
    for number in range(1, len(QUAD)):
        parts[number] = exchange(parts[number], n, tuple(2 * m for m in QUAD[number]))
    for bit in range(2, (n // 2).bit_length() - 1):
        width //= 2
        send, keep = pl.pallas_call(
            functools.partial(halve_kernel, piece, bit),
            out_shape=[jax.ShapeDtypeStruct((width, CW), jnp.float32)] * 2,
            in_specs=[VMEM] * len(parts),
            out_specs=[VMEM] * 2,
            compiler_params=params(2),
            name=f"halve{bit}",
        )(*parts)
        got = exchange(send, n, (2 << bit, 2 << bit))
        parts = [keep, got]
    child_diag = pl.pallas_call(
        last_kernel,
        out_shape=jax.ShapeDtypeStruct((piece, CW), jnp.float32),
        in_specs=[VMEM] * 4,
        out_specs=VMEM,
        compiler_params=params(2),
        name="last",
    )(child_inverse, keep, got, token)
    return offdiag, child_diag


def solution(mesh):
    split = P(("pole", "row"), None)
    return jax.shard_map(
        functools.partial(per_device, mesh.shape["row"]),
        mesh=mesh,
        in_specs=(split, split, P(), split),
        out_specs=(split, split),
        check_vma=False,
    )
```

```python
import functools

import jax
import jax.numpy as jnp
from jax import lax
from jax.experimental import pallas as pl
from jax.experimental.pallas import tpu as pltpu
from jax.sharding import PartitionSpec as P

NCH = 2
CW = 256
MIB = 2**20
EARLY = ("own", "a", "d")
PASSES = 3
QUAD = ((0, 0), (1, 2), (2, 1), (3, 3))
SMEM = pl.BlockSpec(memory_space=pltpu.SMEM)
VMEM = pl.BlockSpec(memory_space=pltpu.VMEM)
ANY = pl.BlockSpec(memory_space=pl.ANY)
TOKEN = pltpu.VMEM((8, 128), jnp.float32)


def params(mib):
    return pltpu.CompilerParams(vmem_limit_bytes=mib * MIB)


def exchange(block, n, masks):
    return lax.ppermute(block, "row", [(i, i ^ masks[i % 2]) for i in range(n)])


def compact_kernel(coupling_ref, panel_ref, block_ref):
    child = coupling_ref[lax.axis_index("row")]
    start = pl.multiple_of(jnp.minimum(child, NCH - 1) * CW, CW)
    block_ref[...] = panel_ref[:, pl.ds(start, CW)]


def load_kernel(mine_hbm, other_hbm, mine_ref, other_ref, sems):
    rows = mine_hbm.shape[0]
    core = lax.rem(lax.axis_index("row"), 2)
    copies = []
    for pair in range(mine_ref.shape[1] // rows):
        here = pl.ds(pl.multiple_of((2 * pair + core) * rows, rows), rows)
        there = pl.ds(pair * rows, rows)
        for number, (source, ref) in enumerate(
            ((mine_hbm, mine_ref), (other_hbm, other_ref))
        ):
            copies.append(
                pltpu.make_async_copy(
                    source.at[:, here], ref.at[:, there], sems.at[pair, number]
                )
            )
    for copy in copies:
        copy.start()
    for copy in copies:
        copy.wait()


def join_kernel(low_ref, high_ref, out_ref):
    rows = low_ref.shape[0]
    out_ref[:rows] = low_ref[...]
    out_ref[rows:] = high_ref[...]


def accumulate(places, coupling_ref, z_refs, block_refs, total_refs):
    rows = z_refs[0].shape[0]
    me = lax.axis_index("row")
    core = lax.rem(me, 2)
    children = (coupling_ref[me], coupling_ref[me ^ 1])
    for held, block_ref in zip(places, block_refs):
        for number, (even, odd) in enumerate(held):
            tile = me ^ jnp.where(core == 0, even, odd)
            tile_child = coupling_ref[tile]
            columns = pl.ds(pl.multiple_of(lax.div(tile, 2) * rows, rows), rows)
            for child, z_ref, total_ref in zip(children, z_refs, total_refs):

                @pl.when((tile_child == child) & (child < NCH))
                def _():
                    total_ref[...] += jnp.dot(
                        z_ref[:, columns],
                        block_ref[number * rows:(number + 1) * rows],
                        preferred_element_type=jnp.float32,
                    )

    return core, children


def early_kernel(places, coupling_ref, mine_z, other_z, other_own, own_ref, *refs):
    block_refs = refs[:-4]
    mine_ref, other_ref, own_t, other_t = refs[-4:]
    own_t[...] = own_ref[...].T
    other_t[...] = other_own[...].T
    for total_ref in (mine_ref, other_ref):
        total_ref[...] = jnp.zeros_like(total_ref)
    accumulate(places, coupling_ref, (mine_z, other_z), block_refs, (mine_ref, other_ref))


def product_kernel(n, places, coupling_ref, mine_z, other_z, *refs):
    mine_part, other_part, own_t, other_t = refs[:4]
    mine_ref, other_ref, send_ref, keep_ref = refs[-4:]
    mine_ref[...] = mine_part[...]
    other_ref[...] = other_part[...]
    core, children = accumulate(
        places, coupling_ref, (mine_z, other_z), refs[4:-4], (mine_ref, other_ref)
    )
    terms = []
    for left_ref, total_ref in ((own_t, mine_ref), (other_t, other_ref)):
        rest = total_ref[...]
        term = jnp.zeros((CW, CW), jnp.float32)
        for _ in range(PASSES):
            part = rest.astype(jnp.bfloat16)
            rest = rest - part.astype(jnp.float32)
            term += jnp.dot(left_ref[...], part, preferred_element_type=jnp.float32)
        terms.append(term)
    piece = NCH * CW // n
    zero = jnp.zeros((piece, CW), jnp.float32)
    for child in range(NCH):
        for q in range(CW // piece // 2):
            low, high = [
                sum(
                    jnp.where(mine == child, term[at:at + piece], zero)
                    for mine, term in zip(children, terms)
                )
                for at in (2 * q * piece, (2 * q + 1) * piece)
            ]
            at = child * (CW // 2) + q * piece
            keep_ref[at:at + piece] = jnp.where(core == 0, low, high)
            send_ref[at:at + piece] = jnp.where(core == 0, high, low)


def offdiag_kernel(coupling_ref, mine_ref, other_ref, offdiag_ref, token_ref):
    token_ref[...] = jnp.zeros_like(token_ref)
    child = coupling_ref[lax.axis_index("row")]
    product = mine_ref[...] + other_ref[...]
    for k in range(NCH):
        offdiag_ref[:, k * CW:(k + 1) * CW] = jnp.where(
            child == k, -product, jnp.zeros_like(product)
        )


def quad_kernel(piece, kept_ref, got_ref, *out_refs):
    me = lax.axis_index("row")
    core = lax.rem(me, 2)
    low = lax.rem(lax.div(me, 2), 4)
    for (even, odd), out_ref in zip(QUAD, out_refs):
        want = low ^ jnp.where(core == 0, even, odd)
        for group in range(out_ref.shape[0] // piece):
            rows = pl.ds(pl.multiple_of((group * 4 + want) * piece, piece), piece)
            out_ref[group * piece:(group + 1) * piece] = kept_ref[rows] + got_ref[rows]


def halve_kernel(piece, bit, *refs):
    part_refs, send_ref, keep_ref = refs[:-2], refs[-2], refs[-1]
    mine = lax.rem(lax.div(lax.axis_index("row"), 2 << bit), 2)
    for out_ref, side in ((keep_ref, mine), (send_ref, 1 - mine)):
        for index in range(out_ref.shape[0] // piece):
            rows = pl.ds(pl.multiple_of((2 * index + side) * piece, piece), piece)
            total = part_refs[0][rows]
            for part_ref in part_refs[1:]:
                total = total + part_ref[rows]
            out_ref[index * piece:(index + 1) * piece] = total


def last_kernel(inverse_ref, kept_ref, got_ref, after_ref, diag_ref):
    diag_ref[...] = inverse_ref[...] + (kept_ref[...] + got_ref[...])


def gather(block, inverse_root, n):
    rows = block.shape[0]
    held = {"own": ([(0, 0)], block)}

    def fetch(name, source, masks):
        tiles, held_block = held[source]
        held[name] = (
            [tuple(masks[c] ^ pair[c] for c in range(2)) for pair in tiles],
            exchange(held_block, n, masks),
        )

    fetch("d", "own", (8, 8))
    other_own = exchange(block, n, (1, 1))
    fetch("a", "own", (2, 4))
    other_z = exchange(lax.optimization_barrier((inverse_root, block))[0], n, (1, 1))
    half = pltpu.VMEM((rows, inverse_root.shape[1] // 2), inverse_root.dtype)
    mine_z, other_z = pl.pallas_call(
        load_kernel,
        out_shape=[half, half],
        in_specs=[ANY, ANY],
        out_specs=[VMEM] * 2,
        scratch_shapes=[pltpu.SemaphoreType.DMA((n // 2, 2))],
        compiler_params=params(60 - inverse_root.size * 2 // MIB),
        name="load",
    )(inverse_root, other_z)
    pair = pl.pallas_call(
        join_kernel,
        out_shape=pltpu.VMEM((2 * rows, CW), block.dtype),
        in_specs=[VMEM, VMEM],
        out_specs=VMEM,
        compiler_params=params(2),
        name="join",
    )(block, held["a"][1])
    held["pair"] = (held["own"][0] + held["a"][0], pair)
    fetch("bc", "pair", (4, 2))
    del held["pair"]
    fetch("g", "d", (6, 6))
    fetch("f", "d", (2, 4))
    fetch("e", "d", (4, 2))
    for bit in range(4, n.bit_length() - 1):
        for name in list(held):
            fetch(f"{name}_{bit}", name, (1 << bit, 1 << bit))
    return mine_z, other_z, other_own, held


def per_device(n, inverse_root, lower_panel, coupling, child_inverse):
    rows = inverse_root.shape[0]
    block = pl.pallas_call(
        compact_kernel,
        out_shape=pltpu.VMEM((rows, CW), lower_panel.dtype),
        in_specs=[SMEM, VMEM],
        out_specs=VMEM,
        compiler_params=params(60),
        name="compact",
    )(coupling, lower_panel)
    mine_z, other_z, other_own, held = gather(block, inverse_root, n)
    late = [name for name in held if name not in EARLY]
    square = jax.ShapeDtypeStruct((rows, CW), jnp.float32)
    turned = jax.ShapeDtypeStruct((CW, rows), block.dtype)
    partial = pl.pallas_call(
        functools.partial(early_kernel, [held[name][0] for name in EARLY]),
        out_shape=[square, square, turned, turned],
        in_specs=[SMEM] + [VMEM] * (len(EARLY) + 4),
        out_specs=[VMEM] * 4,
        compiler_params=params(24 if n > 16 else 8),
        name="early",
    )(coupling, mine_z, other_z, other_own, block, *[held[name][1] for name in EARLY])
    mine, other, send, keep = pl.pallas_call(
        functools.partial(product_kernel, n, [held[name][0] for name in late]),
        out_shape=[square, square]
        + [jax.ShapeDtypeStruct((NCH * CW // 2, CW), jnp.float32)] * 2,
        in_specs=[SMEM] + [VMEM] * (len(late) + 6),
        out_specs=[VMEM] * 4,
        compiler_params=params(24 if n > 16 else 8),
        name="product",
    )(
        coupling,
        mine_z,
        other_z,
        *partial,
        *[held[name][1] for name in late],
    )
    got = exchange(send, n, (1, 1))
    piece = NCH * CW // n
    width = NCH * CW // 2 // len(QUAD)
    parts = list(pl.pallas_call(
        functools.partial(quad_kernel, piece),
        out_shape=[jax.ShapeDtypeStruct((width, CW), jnp.float32)] * len(QUAD),
        in_specs=[VMEM] * 2,
        out_specs=[VMEM] * len(QUAD),
        compiler_params=params(2),
        name="quad",
    )(keep, got))
    for number in range(1, len(QUAD)):
        parts[number] = exchange(parts[number], n, tuple(2 * m for m in QUAD[number]))
    for bit in range(2, (n // 2).bit_length() - 1):
        width //= 2
        send, keep = pl.pallas_call(
            functools.partial(halve_kernel, piece, bit),
            out_shape=[jax.ShapeDtypeStruct((width, CW), jnp.float32)] * 2,
            in_specs=[VMEM] * len(parts),
            out_specs=[VMEM] * 2,
            compiler_params=params(2),
            name=f"halve{bit}",
        )(*parts)
        got = exchange(send, n, (2 << bit, 2 << bit))
        parts = [keep, got]
    offdiag, token = pl.pallas_call(
        offdiag_kernel,
        out_shape=[jax.ShapeDtypeStruct((rows, NCH * CW), jnp.float32), TOKEN],
        in_specs=[SMEM, VMEM, VMEM],
        out_specs=[VMEM] * 2,
        compiler_params=params(4),
        name="offdiag",
    )(coupling, mine, exchange(other, n, (1, 1)))
    child_diag = pl.pallas_call(
        last_kernel,
        out_shape=jax.ShapeDtypeStruct((piece, CW), jnp.float32),
        in_specs=[VMEM] * 4,
        out_specs=VMEM,
        compiler_params=params(2),
        name="last",
    )(child_inverse, keep, got, token)
    return offdiag, child_diag


def solution(mesh):
    split = P(("pole", "row"), None)
    return jax.shard_map(
        functools.partial(per_device, mesh.shape["row"]),
        mesh=mesh,
        in_specs=(split, split, P(), split),
        out_specs=(split, split),
        check_vma=False,
    )
```

```python
import functools

import jax
import jax.numpy as jnp
from jax import lax
from jax.experimental import pallas as pl
from jax.experimental.pallas import tpu as pltpu
from jax.sharding import PartitionSpec as P

NCH = 2
CW = 256
MIB = 2**20
EARLY = ("own", "a", "d")
PASSES = 3
QUAD = ((0, 0), (3, 3), (1, 2), (2, 1))
BITS = 24
SMEM = pl.BlockSpec(memory_space=pltpu.SMEM)
VMEM = pl.BlockSpec(memory_space=pltpu.VMEM)
ANY = pl.BlockSpec(memory_space=pl.ANY)
TOKEN = pltpu.VMEM((8, 128), jnp.float32)


def params(mib):
    return pltpu.CompilerParams(vmem_limit_bytes=mib * MIB)


def exchange(block, n, masks):
    return lax.ppermute(block, "row", [(i, i ^ masks[i % 2]) for i in range(n)])


def compact_kernel(coupling_ref, panel_ref, block_ref):
    child = coupling_ref[lax.axis_index("row")]
    start = pl.multiple_of(jnp.minimum(child, NCH - 1) * CW, CW)
    block_ref[...] = panel_ref[:, pl.ds(start, CW)]


def load_kernel(mine_hbm, other_hbm, mine_ref, other_ref, sems):
    rows = mine_hbm.shape[0]
    core = lax.rem(lax.axis_index("row"), 2)
    copies = []
    for pair in range(mine_ref.shape[1] // rows):
        here = pl.ds(pl.multiple_of((2 * pair + core) * rows, rows), rows)
        there = pl.ds(pair * rows, rows)
        for number, (source, ref) in enumerate(
            ((mine_hbm, mine_ref), (other_hbm, other_ref))
        ):
            copies.append(
                pltpu.make_async_copy(
                    source.at[:, here], ref.at[:, there], sems.at[pair, number]
                )
            )
    for copy in copies:
        copy.start()
    for copy in copies:
        copy.wait()


def join_kernel(low_ref, high_ref, out_ref):
    rows = low_ref.shape[0]
    out_ref[:rows] = low_ref[...]
    out_ref[rows:] = high_ref[...]


def walk(places, block_refs):
    me = lax.axis_index("row")
    core = lax.rem(me, 2)
    for held, block_ref in zip(places, block_refs):
        for number, (even, odd) in enumerate(held):
            yield me ^ jnp.where(core == 0, even, odd), number, block_ref


def accumulate(places, wanted, z_refs, block_refs, total_refs):
    rows = z_refs[0].shape[0]
    for at, (tile, number, block_ref) in enumerate(walk(places, block_refs)):
        columns = pl.ds(pl.multiple_of(lax.div(tile, 2) * rows, rows), rows)
        for side, (z_ref, total_ref) in enumerate(zip(z_refs, total_refs)):

            @pl.when(wanted(at, side, tile))
            def _():
                total_ref[...] += jnp.dot(
                    z_ref[:, columns],
                    block_ref[number * rows:(number + 1) * rows],
                    preferred_element_type=jnp.float32,
                )


def early_kernel(
    places, late_places, coupling_ref, mine_z, other_z, other_own, own_ref, *refs
):
    block_refs = refs[:-5]
    mine_ref, other_ref, own_t, other_t, flag_ref = refs[-5:]
    me = lax.axis_index("row")
    children = (coupling_ref[me], coupling_ref[me ^ 1])

    def wanted(_, side, tile):
        return (coupling_ref[tile] == children[side]) & (children[side] < NCH)

    flags = [children[side] == child for child in range(NCH) for side in range(2)]
    for tile, _, _ in walk(late_places, late_places):
        flags += [wanted(None, side, tile) for side in range(2)]
    for word in range(flag_ref.shape[0]):
        value = jnp.int32(0)
        for bit, flag in enumerate(flags[word * BITS:(word + 1) * BITS]):
            value = value + jnp.where(flag, 1 << bit, 0)
        flag_ref[word:word + 1] = jnp.full((1, 128), value, jnp.int32)
    own_t[...] = own_ref[...].T
    other_t[...] = other_own[...].T
    for total_ref in (mine_ref, other_ref):
        total_ref[...] = jnp.zeros_like(total_ref)
    accumulate(places, wanted, (mine_z, other_z), block_refs, (mine_ref, other_ref))


def product_kernel(n, places, mine_z, other_z, *refs):
    mine_part, other_part, own_t, other_t, flag_ref = refs[:5]
    mine_ref, other_ref, send_ref, keep_ref = refs[-4:]
    count = 2 * (NCH + sum(len(held) for held in places))
    words = [jnp.max(flag_ref[word:word + 1]) for word in range(-(-count // BITS))]
    flags = [lax.rem(words[at // BITS] >> (at % BITS), 2) == 1 for at in range(count)]
    mine_ref[...] = mine_part[...]
    other_ref[...] = other_part[...]
    accumulate(
        places,
        lambda at, side, _: flags[2 * (NCH + at) + side],
        (mine_z, other_z),
        refs[5:-4],
        (mine_ref, other_ref),
    )
    core = lax.rem(lax.axis_index("row"), 2)
    terms = []
    for left_ref, total_ref in ((own_t, mine_ref), (other_t, other_ref)):
        rest = total_ref[...]
        term = jnp.zeros((CW, CW), jnp.float32)
        for _ in range(PASSES):
            part = rest.astype(jnp.bfloat16)
            rest = rest - part.astype(jnp.float32)
            term += jnp.dot(left_ref[...], part, preferred_element_type=jnp.float32)
        terms.append(term)
    piece = NCH * CW // n
    zero = jnp.zeros((piece, CW), jnp.float32)
    for child in range(NCH):
        for q in range(CW // piece // 2):
            low, high = [
                sum(
                    jnp.where(flags[2 * child + side], term[at:at + piece], zero)
                    for side, term in enumerate(terms)
                )
                for at in (2 * q * piece, (2 * q + 1) * piece)
            ]
            at = child * (CW // 2) + q * piece
            keep_ref[at:at + piece] = jnp.where(core == 0, low, high)
            send_ref[at:at + piece] = jnp.where(core == 0, high, low)


def offdiag_kernel(coupling_ref, mine_ref, other_ref, offdiag_ref, token_ref):
    token_ref[...] = jnp.zeros_like(token_ref)
    child = coupling_ref[lax.axis_index("row")]
    product = mine_ref[...] + other_ref[...]
    for k in range(NCH):
        offdiag_ref[:, k * CW:(k + 1) * CW] = jnp.where(
            child == k, -product, jnp.zeros_like(product)
        )


def quad_kernel(piece, kept_ref, got_ref, *out_refs):
    me = lax.axis_index("row")
    core = lax.rem(me, 2)
    low = lax.rem(lax.div(me, 2), 4)
    for (even, odd), out_ref in zip(QUAD, out_refs):
        want = low ^ jnp.where(core == 0, even, odd)
        for group in range(out_ref.shape[0] // piece):
            rows = pl.ds(pl.multiple_of((group * 4 + want) * piece, piece), piece)
            out_ref[group * piece:(group + 1) * piece] = kept_ref[rows] + got_ref[rows]


def halve_kernel(piece, bit, *refs):
    part_refs, send_ref, keep_ref = refs[:-2], refs[-2], refs[-1]
    mine = lax.rem(lax.div(lax.axis_index("row"), 2 << bit), 2)
    for out_ref, side in ((keep_ref, mine), (send_ref, 1 - mine)):
        for index in range(out_ref.shape[0] // piece):
            rows = pl.ds(pl.multiple_of((2 * index + side) * piece, piece), piece)
            total = part_refs[0][rows]
            for part_ref in part_refs[1:]:
                total = total + part_ref[rows]
            out_ref[index * piece:(index + 1) * piece] = total


def last_kernel(inverse_ref, kept_ref, got_ref, after_ref, diag_ref):
    diag_ref[...] = inverse_ref[...] + (kept_ref[...] + got_ref[...])


def gather(block, inverse_root, n):
    rows = block.shape[0]
    held = {"own": ([(0, 0)], block)}

    def fetch(name, source, masks):
        tiles, held_block = held[source]
        held[name] = (
            [tuple(masks[c] ^ pair[c] for c in range(2)) for pair in tiles],
            exchange(held_block, n, masks),
        )

    fetch("d", "own", (8, 8))
    other_own = exchange(block, n, (1, 1))
    fetch("a", "own", (2, 4))
    other_z = exchange(lax.optimization_barrier((inverse_root, block))[0], n, (1, 1))
    half = pltpu.VMEM((rows, inverse_root.shape[1] // 2), inverse_root.dtype)
    mine_z, other_z = pl.pallas_call(
        load_kernel,
        out_shape=[half, half],
        in_specs=[ANY, ANY],
        out_specs=[VMEM] * 2,
        scratch_shapes=[pltpu.SemaphoreType.DMA((n // 2, 2))],
        compiler_params=params(60 - inverse_root.size * 2 // MIB),
        name="load",
    )(inverse_root, other_z)
    pair = pl.pallas_call(
        join_kernel,
        out_shape=pltpu.VMEM((2 * rows, CW), block.dtype),
        in_specs=[VMEM, VMEM],
        out_specs=VMEM,
        compiler_params=params(2),
        name="join",
    )(block, held["a"][1])
    held["pair"] = (held["own"][0] + held["a"][0], pair)
    fetch("bc", "pair", (4, 2))
    del held["pair"]
    fetch("g", "d", (6, 6))
    fetch("f", "d", (2, 4))
    fetch("e", "d", (4, 2))
    for bit in range(4, n.bit_length() - 1):
        for name in list(held):
            fetch(f"{name}_{bit}", name, (1 << bit, 1 << bit))
    return mine_z, other_z, other_own, held


def per_device(n, inverse_root, lower_panel, coupling, child_inverse):
    rows = inverse_root.shape[0]
    block = pl.pallas_call(
        compact_kernel,
        out_shape=pltpu.VMEM((rows, CW), lower_panel.dtype),
        in_specs=[SMEM, VMEM],
        out_specs=VMEM,
        compiler_params=params(60),
        name="compact",
    )(coupling, lower_panel)
    mine_z, other_z, other_own, held = gather(block, inverse_root, n)
    late = [name for name in held if name not in EARLY]
    square = jax.ShapeDtypeStruct((rows, CW), jnp.float32)
    turned = jax.ShapeDtypeStruct((CW, rows), block.dtype)
    late_places = [held[name][0] for name in late]
    count = 2 * (NCH + sum(len(tiles) for tiles in late_places))
    partial = pl.pallas_call(
        functools.partial(
            early_kernel, [held[name][0] for name in EARLY], late_places
        ),
        out_shape=[
            square,
            square,
            turned,
            turned,
            jax.ShapeDtypeStruct((-(-count // BITS), 128), jnp.int32),
        ],
        in_specs=[SMEM] + [VMEM] * (len(EARLY) + 4),
        out_specs=[VMEM] * 5,
        compiler_params=params(24 if n > 16 else 8),
        name="early",
    )(coupling, mine_z, other_z, other_own, block, *[held[name][1] for name in EARLY])
    mine, other, send, keep = pl.pallas_call(
        functools.partial(product_kernel, n, late_places),
        out_shape=[square, square]
        + [jax.ShapeDtypeStruct((NCH * CW // 2, CW), jnp.float32)] * 2,
        in_specs=[VMEM] * (len(late) + 7),
        out_specs=[VMEM] * 4,
        compiler_params=params(24 if n > 16 else 8),
        name="product",
    )(mine_z, other_z, *partial, *[held[name][1] for name in late])
    got = exchange(send, n, (1, 1))
    piece = NCH * CW // n
    width = NCH * CW // 2 // len(QUAD)
    parts = list(pl.pallas_call(
        functools.partial(quad_kernel, piece),
        out_shape=[jax.ShapeDtypeStruct((width, CW), jnp.float32)] * len(QUAD),
        in_specs=[VMEM] * 2,
        out_specs=[VMEM] * len(QUAD),
        compiler_params=params(2),
        name="quad",
    )(keep, got))
    for number in range(1, len(QUAD)):
        parts[number] = exchange(parts[number], n, tuple(2 * m for m in QUAD[number]))
    for bit in range(2, (n // 2).bit_length() - 1):
        width //= 2
        send, keep = pl.pallas_call(
            functools.partial(halve_kernel, piece, bit),
            out_shape=[jax.ShapeDtypeStruct((width, CW), jnp.float32)] * 2,
            in_specs=[VMEM] * len(parts),
            out_specs=[VMEM] * 2,
            compiler_params=params(2),
            name=f"halve{bit}",
        )(*parts)
        got = exchange(send, n, (2 << bit, 2 << bit))
        parts = [keep, got]
    offdiag, token = pl.pallas_call(
        offdiag_kernel,
        out_shape=[jax.ShapeDtypeStruct((rows, NCH * CW), jnp.float32), TOKEN],
        in_specs=[SMEM, VMEM, VMEM],
        out_specs=[VMEM] * 2,
        compiler_params=params(4),
        name="offdiag",
    )(coupling, mine, exchange(other, n, (1, 1)))
    child_diag = pl.pallas_call(
        last_kernel,
        out_shape=jax.ShapeDtypeStruct((piece, CW), jnp.float32),
        in_specs=[VMEM] * 4,
        out_specs=VMEM,
        compiler_params=params(2),
        name="last",
    )(child_inverse, keep, got, token)
    return offdiag, child_diag


def solution(mesh):
    split = P(("pole", "row"), None)
    return jax.shard_map(
        functools.partial(per_device, mesh.shape["row"]),
        mesh=mesh,
        in_specs=(split, split, P(), split),
        out_specs=(split, split),
        check_vma=False,
    )
```

```python
import functools

import jax
import jax.numpy as jnp
from jax import lax
from jax.experimental import pallas as pl
from jax.experimental.pallas import tpu as pltpu
from jax.sharding import PartitionSpec as P

NCH = 2
CW = 256
MIB = 2**20
EARLY = ("own", "a", "d")
PASSES = 3
QUAD = ((0, 0), (3, 3), (1, 2), (2, 1))
BITS = 24
SMEM = pl.BlockSpec(memory_space=pltpu.SMEM)
VMEM = pl.BlockSpec(memory_space=pltpu.VMEM)
ANY = pl.BlockSpec(memory_space=pl.ANY)
TOKEN = pltpu.VMEM((8, 128), jnp.float32)


def params(mib):
    return pltpu.CompilerParams(vmem_limit_bytes=mib * MIB)


def exchange(block, n, masks):
    return lax.ppermute(block, "row", [(i, i ^ masks[i % 2]) for i in range(n)])


def compact_kernel(coupling_ref, panel_ref, block_ref):
    child = coupling_ref[lax.axis_index("row")]
    start = pl.multiple_of(jnp.minimum(child, NCH - 1) * CW, CW)
    block_ref[...] = panel_ref[:, pl.ds(start, CW)]


def load_kernel(mine_hbm, other_hbm, mine_ref, other_ref, sems):
    rows = mine_hbm.shape[0]
    core = lax.rem(lax.axis_index("row"), 2)
    copies = []
    for pair in range(mine_ref.shape[1] // rows):
        here = pl.ds(pl.multiple_of((2 * pair + core) * rows, rows), rows)
        there = pl.ds(pair * rows, rows)
        for number, (source, ref) in enumerate(
            ((mine_hbm, mine_ref), (other_hbm, other_ref))
        ):
            copies.append(
                pltpu.make_async_copy(
                    source.at[:, here], ref.at[:, there], sems.at[pair, number]
                )
            )
    for copy in copies:
        copy.start()
    for copy in copies:
        copy.wait()


def join_kernel(low_ref, high_ref, out_ref):
    rows = low_ref.shape[0]
    out_ref[:rows] = low_ref[...]
    out_ref[rows:] = high_ref[...]


def walk(places, block_refs):
    me = lax.axis_index("row")
    core = lax.rem(me, 2)
    for held, block_ref in zip(places, block_refs):
        for number, (even, odd) in enumerate(held):
            yield me ^ jnp.where(core == 0, even, odd), number, block_ref


def accumulate(places, wanted, z_refs, block_refs, total_refs):
    rows = z_refs[0].shape[0]
    for at, (tile, number, block_ref) in enumerate(walk(places, block_refs)):
        columns = pl.ds(pl.multiple_of(lax.div(tile, 2) * rows, rows), rows)
        for side, (z_ref, total_ref) in enumerate(zip(z_refs, total_refs)):

            @pl.when(wanted(at, side, tile))
            def _():
                total_ref[...] += jnp.dot(
                    z_ref[:, columns],
                    block_ref[number * rows:(number + 1) * rows],
                    preferred_element_type=jnp.float32,
                )


def early_kernel(
    places, late_places, coupling_ref, mine_z, other_z, other_own, own_ref, *refs
):
    block_refs = refs[:-5]
    mine_ref, other_ref, own_t, other_t, flag_ref = refs[-5:]
    me = lax.axis_index("row")
    children = (coupling_ref[me], coupling_ref[me ^ 1])

    def wanted(_, side, tile):
        return (coupling_ref[tile] == children[side]) & (children[side] < NCH)

    flags = [children[side] == child for child in range(NCH) for side in range(2)]
    for tile, _, _ in walk(late_places, late_places):
        flags += [wanted(None, side, tile) for side in range(2)]
    for word in range(flag_ref.shape[0]):
        value = jnp.int32(0)
        for bit, flag in enumerate(flags[word * BITS:(word + 1) * BITS]):
            value = value + jnp.where(flag, 1 << bit, 0)
        flag_ref[word:word + 1] = jnp.full((1, 128), value, jnp.int32)
    own_t[...] = own_ref[...].T
    other_t[...] = other_own[...].T
    for total_ref in (mine_ref, other_ref):
        total_ref[...] = jnp.zeros_like(total_ref)
    accumulate(places, wanted, (mine_z, other_z), block_refs, (mine_ref, other_ref))


def product_kernel(n, places, mine_z, other_z, *refs):
    mine_part, other_part, own_t, other_t, flag_ref = refs[:5]
    mine_ref, other_ref, send_ref, keep_ref = refs[-4:]
    count = 2 * (NCH + sum(len(held) for held in places))
    words = [jnp.max(flag_ref[word:word + 1]) for word in range(-(-count // BITS))]
    flags = [lax.rem(words[at // BITS] >> (at % BITS), 2) == 1 for at in range(count)]
    mine_ref[...] = mine_part[...]
    other_ref[...] = other_part[...]
    accumulate(
        places,
        lambda at, side, _: flags[2 * (NCH + at) + side],
        (mine_z, other_z),
        refs[5:-4],
        (mine_ref, other_ref),
    )
    core = lax.rem(lax.axis_index("row"), 2)
    terms = []
    for left_ref, total_ref in ((own_t, mine_ref), (other_t, other_ref)):
        rest = total_ref[...]
        term = jnp.zeros((CW, CW), jnp.float32)
        for _ in range(PASSES):
            part = rest.astype(jnp.bfloat16)
            rest = rest - part.astype(jnp.float32)
            term += jnp.dot(left_ref[...], part, preferred_element_type=jnp.float32)
        terms.append(term)
    piece = NCH * CW // n
    zero = jnp.zeros((piece, CW), jnp.float32)
    for child in range(NCH):
        for q in range(CW // piece // 2):
            low, high = [
                sum(
                    jnp.where(flags[2 * child + side], term[at:at + piece], zero)
                    for side, term in enumerate(terms)
                )
                for at in (2 * q * piece, (2 * q + 1) * piece)
            ]
            at = child * (CW // 2) + q * piece
            keep_ref[at:at + piece] = jnp.where(core == 0, low, high)
            send_ref[at:at + piece] = jnp.where(core == 0, high, low)


def offdiag_kernel(coupling_ref, mine_ref, other_ref, offdiag_ref, token_ref):
    token_ref[...] = jnp.zeros_like(token_ref)
    child = coupling_ref[lax.axis_index("row")]
    product = mine_ref[...] + other_ref[...]
    for k in range(NCH):
        offdiag_ref[:, k * CW:(k + 1) * CW] = jnp.where(
            child == k, -product, jnp.zeros_like(product)
        )


def quad_kernel(piece, kept_ref, got_ref, *out_refs):
    me = lax.axis_index("row")
    core = lax.rem(me, 2)
    low = lax.rem(lax.div(me, 2), 4)
    for (even, odd), out_ref in zip(QUAD, out_refs):
        want = low ^ jnp.where(core == 0, even, odd)
        for group in range(out_ref.shape[0] // piece):
            rows = pl.ds(pl.multiple_of((group * 4 + want) * piece, piece), piece)
            out_ref[group * piece:(group + 1) * piece] = kept_ref[rows] + got_ref[rows]


def halve_kernel(piece, bit, *refs):
    part_refs, send_ref, keep_ref = refs[:-2], refs[-2], refs[-1]
    mine = lax.rem(lax.div(lax.axis_index("row"), 2 << bit), 2)
    for out_ref, side in ((keep_ref, mine), (send_ref, 1 - mine)):
        for index in range(out_ref.shape[0] // piece):
            rows = pl.ds(pl.multiple_of((2 * index + side) * piece, piece), piece)
            total = part_refs[0][rows]
            for part_ref in part_refs[1:]:
                total = total + part_ref[rows]
            out_ref[index * piece:(index + 1) * piece] = total


def last_kernel(inverse_ref, kept_ref, got_ref, after_ref, diag_ref):
    diag_ref[...] = inverse_ref[...] + (kept_ref[...] + got_ref[...])


def gather(block, inverse_root, n):
    rows = block.shape[0]
    held = {"own": ([(0, 0)], block)}

    def fetch(name, source, masks):
        tiles, held_block = held[source]
        held[name] = (
            [tuple(masks[c] ^ pair[c] for c in range(2)) for pair in tiles],
            exchange(held_block, n, masks),
        )

    fetch("d", "own", (12, 12))
    other_own = exchange(block, n, (1, 1))
    fetch("a", "own", (4, 2))
    other_z = exchange(lax.optimization_barrier((inverse_root, block))[0], n, (1, 1))
    half = pltpu.VMEM((rows, inverse_root.shape[1] // 2), inverse_root.dtype)
    mine_z, other_z = pl.pallas_call(
        load_kernel,
        out_shape=[half, half],
        in_specs=[ANY, ANY],
        out_specs=[VMEM] * 2,
        scratch_shapes=[pltpu.SemaphoreType.DMA((n // 2, 2))],
        compiler_params=params(60 - inverse_root.size * 2 // MIB),
        name="load",
    )(inverse_root, other_z)
    pair = pl.pallas_call(
        join_kernel,
        out_shape=pltpu.VMEM((2 * rows, CW), block.dtype),
        in_specs=[VMEM, VMEM],
        out_specs=VMEM,
        compiler_params=params(2),
        name="join",
    )(block, held["a"][1])
    held["pair"] = (held["own"][0] + held["a"][0], pair)
    fetch("bc", "pair", (2, 4))
    del held["pair"]
    fetch("g", "d", (6, 6))
    fetch("f", "d", (4, 2))
    fetch("e", "d", (2, 4))
    for bit in range(4, n.bit_length() - 1):
        for name in list(held):
            fetch(f"{name}_{bit}", name, (1 << bit, 1 << bit))
    return mine_z, other_z, other_own, held


def per_device(n, inverse_root, lower_panel, coupling, child_inverse):
    rows = inverse_root.shape[0]
    block = pl.pallas_call(
        compact_kernel,
        out_shape=pltpu.VMEM((rows, CW), lower_panel.dtype),
        in_specs=[SMEM, VMEM],
        out_specs=VMEM,
        compiler_params=params(60),
        name="compact",
    )(coupling, lower_panel)
    mine_z, other_z, other_own, held = gather(block, inverse_root, n)
    late = [name for name in held if name not in EARLY]
    square = jax.ShapeDtypeStruct((rows, CW), jnp.float32)
    turned = jax.ShapeDtypeStruct((CW, rows), block.dtype)
    late_places = [held[name][0] for name in late]
    count = 2 * (NCH + sum(len(tiles) for tiles in late_places))
    partial = pl.pallas_call(
        functools.partial(
            early_kernel, [held[name][0] for name in EARLY], late_places
        ),
        out_shape=[
            square,
            square,
            turned,
            turned,
            jax.ShapeDtypeStruct((-(-count // BITS), 128), jnp.int32),
        ],
        in_specs=[SMEM] + [VMEM] * (len(EARLY) + 4),
        out_specs=[VMEM] * 5,
        compiler_params=params(24 if n > 16 else 8),
        name="early",
    )(coupling, mine_z, other_z, other_own, block, *[held[name][1] for name in EARLY])
    mine, other, send, keep = pl.pallas_call(
        functools.partial(product_kernel, n, late_places),
        out_shape=[square, square]
        + [jax.ShapeDtypeStruct((NCH * CW // 2, CW), jnp.float32)] * 2,
        in_specs=[VMEM] * (len(late) + 7),
        out_specs=[VMEM] * 4,
        compiler_params=params(24 if n > 16 else 8),
        name="product",
    )(mine_z, other_z, *partial, *[held[name][1] for name in late])
    got = exchange(send, n, (1, 1))
    piece = NCH * CW // n
    width = NCH * CW // 2 // len(QUAD)
    parts = list(pl.pallas_call(
        functools.partial(quad_kernel, piece),
        out_shape=[jax.ShapeDtypeStruct((width, CW), jnp.float32)] * len(QUAD),
        in_specs=[VMEM] * 2,
        out_specs=[VMEM] * len(QUAD),
        compiler_params=params(2),
        name="quad",
    )(keep, got))
    for number in range(1, len(QUAD)):
        parts[number] = exchange(parts[number], n, tuple(2 * m for m in QUAD[number]))
    for bit in range(2, (n // 2).bit_length() - 1):
        width //= 2
        send, keep = pl.pallas_call(
            functools.partial(halve_kernel, piece, bit),
            out_shape=[jax.ShapeDtypeStruct((width, CW), jnp.float32)] * 2,
            in_specs=[VMEM] * len(parts),
            out_specs=[VMEM] * 2,
            compiler_params=params(2),
            name=f"halve{bit}",
        )(*parts)
        got = exchange(send, n, (2 << bit, 2 << bit))
        parts = [keep, got]
    offdiag, token = pl.pallas_call(
        offdiag_kernel,
        out_shape=[jax.ShapeDtypeStruct((rows, NCH * CW), jnp.float32), TOKEN],
        in_specs=[SMEM, VMEM, VMEM],
        out_specs=[VMEM] * 2,
        compiler_params=params(4),
        name="offdiag",
    )(coupling, mine, exchange(other, n, (1, 1)))
    child_diag = pl.pallas_call(
        last_kernel,
        out_shape=jax.ShapeDtypeStruct((piece, CW), jnp.float32),
        in_specs=[VMEM] * 4,
        out_specs=VMEM,
        compiler_params=params(2),
        name="last",
    )(child_inverse, keep, got, token)
    return offdiag, child_diag


def solution(mesh):
    split = P(("pole", "row"), None)
    return jax.shard_map(
        functools.partial(per_device, mesh.shape["row"]),
        mesh=mesh,
        in_specs=(split, split, P(), split),
        out_specs=(split, split),
        check_vma=False,
    )
```
